1024 devices in a mesh: gx: 32 (over x_hi, y, core), gy: 4 (over x_lo), gz: 8 (over z).
Axes of the slice: x: 8 (x_hi: 2, x_lo: 4; x = x_hi * 4 + x_lo), y: 8, z: 8, core: 2. Of those that a mesh axis runs over, the one named last changes fastest.
Arguments:
- offsets: float32 [64, 8, 16, 3, 128], P('gx', 'gy', 'gz'), may hold values from 0 to 1
- velocity: float32 [64, 8, 16, 3, 128], P('gx', 'gy', 'gz'), may hold values from -6 to 6
- mass: float32 [64, 8, 16, 128], P('gx', 'gy', 'gz'), may hold values from 0.05 to 0.2
- energy: float32 [64, 8, 16, 128], P('gx', 'gy', 'gz'), may hold values from 0.5 to 2
- partner_mask: int32 [64, 8, 16, 27], P('gx', 'gy', 'gz'), may hold values from 0 to 1, as said below
- counts: int32 [64, 8, 16], P('gx', 'gy', 'gz'), may hold values from 1 to 128, as said below
Outputs:
- acceleration: float32 [64, 8, 16, 3, 128], P('gx', 'gy', 'gz')
- energy_rate: float32 [64, 8, 16, 128], P('gx', 'gy', 'gz')
The draws below stay inside these ranges and needn't reach their ends.
Inputs may be any that keep to these rules, and one draw needn't show every extreme that they name: `partner_mask`: partner 13 (the leaf itself) is always 1. `counts`: some leaf holds 128 valid particles.
All inputs are finite; a program needn't handle non-finite values.
Results may differ from the reference program's by a relative error of at most 0.0003.
Values sent between devices are 32-bit elements; how exact they have to be, the bound alone decides.
A program may use at most 32 MiB of HBM per device.

```python
import math
import jax
import jax.numpy as jnp
from jax import lax

P_SIZE = 128
LX = 2
LY = 2
LZ = 2
NLX = 64
NLY = 8
NLZ = 16


def draw_partner_mask(key, part):
    picks = jax.random.randint(key, (NLX, NLY, NLZ, 27), 0, 5)
    own = jnp.arange(27, dtype=jnp.int32) == 13
    kept = (picks < 4).astype(jnp.int32)
    return jnp.where(own[None, None, None, :], 1, kept).astype(jnp.int32)


def draw_counts(key, part):
    first = jax.random.fold_in(key, 11)
    second = jax.random.fold_in(key, 23)
    level = jax.random.randint(first, (NLX // LX, NLY // LY, NLZ // LZ), 0, 4)
    level = jnp.repeat(jnp.repeat(jnp.repeat(level, LX, 0), LY, 1), LZ, 2)
    ceiling = P_SIZE // jnp.left_shift(jnp.ones_like(level), level)
    drawn = 1 + jax.random.randint(second, level.shape, 0, ceiling)
    drawn = drawn.at[0, 0, 0].set(P_SIZE)
    return drawn.astype(jnp.int32)


def block_scale(stream_key, dims, pieces, least, largest):
    level, own = 1.0, jax.random.fold_in(stream_key, 6)
    for position, parts in pieces:
        heights = jnp.exp(jax.random.uniform(jax.random.fold_in(own, position), (parts,), jnp.float32, least / len(pieces), largest / len(pieces)))
        level = level * jnp.repeat(heights, dims[position] // parts).reshape([-1 if axis == position else 1 for axis in range(len(dims))])
    return level


def normal_values(key, dims, spread, bound, shards=(), kind=jnp.bfloat16):
    array = jax.random.normal(key, dims, jnp.float32) * spread
    if len(shards) > 0:
        array = block_scale(key, dims, shards, -0.22, 0.18) * array
    return jnp.clip(array, min=-bound, max=bound).astype(kind)


def setup_inputs(seed: int = 0) -> dict:
    splits = jax.random.split(jax.random.key(seed), 7)
    offsets = jnp.clip(1.0 * jax.random.uniform(splits[0], (NLX, NLY, NLZ, 3, P_SIZE), jnp.float32) ** block_scale(splits[0], (NLX, NLY, NLZ, 3, P_SIZE), ((0, 32), (1, 4), (2, 8)), -0.2, 0.2), 0.0, 1.0)
    velocity = normal_values(splits[1], (NLX, NLY, NLZ, 3, P_SIZE), 1.0, 6.0, ((0, 32), (1, 4), (2, 8)), jnp.float32)
    mass = jnp.clip(jnp.exp(math.log(0.2) - 1.3862944 * jax.random.uniform(splits[2], (NLX, NLY, NLZ, P_SIZE), jnp.float32) ** block_scale(splits[2], (NLX, NLY, NLZ, P_SIZE), ((0, 32), (1, 4), (2, 8)), -0.2, 0.2)), 0.05, 0.2)
    energy = jnp.clip(jnp.exp(math.log(2.0) - 1.3862944 * jax.random.uniform(splits[3], (NLX, NLY, NLZ, P_SIZE), jnp.float32) ** block_scale(splits[3], (NLX, NLY, NLZ, P_SIZE), ((0, 32), (1, 4), (2, 8)), -0.2, 0.2)), 0.5, 2.0)
    partner_mask = draw_partner_mask(jax.random.fold_in(splits[6], 71), 0)
    counts = draw_counts(jax.random.fold_in(splits[6], 71), 0)
    return {"offsets": offsets, "velocity": velocity, "mass": mass, "energy": energy, "partner_mask": partner_mask, "counts": counts}


def pair_geometry(center, partner, shift):
    separation = center[:, :, 0:3, :, None] - partner[:, :, 0:3, None, :] - shift[None, None, :, None, None]
    radius = jnp.sqrt(lax.optimization_barrier(jnp.sum(separation * separation, axis=2)))
    inside = jnp.maximum(1.0 - radius, 0.0)
    cubed = inside * inside * inside
    kernel = cubed * inside * (1.0 + 4.0 * radius)
    slope = -20.0 * cubed
    return (separation, kernel, slope)

def volume_terms(center, partner, shift):
    separation, kernel, slope = pair_geometry(center, partner, shift)
    return lax.optimization_barrier(jnp.sum(kernel * partner[:, :, 3, None, :], axis=-1))[:, :, None, :]

def density_terms(center, partner, shift):
    separation, kernel, slope = pair_geometry(center, partner, shift)
    weight = partner[:, :, 3, None, :]
    mass_far = partner[:, :, 4, None, :]
    volume_far = partner[:, :, 8, None, :]
    summed_mass = lax.optimization_barrier(jnp.sum(weight * mass_far * kernel, axis=-1))
    summed_volume = lax.optimization_barrier(jnp.sum(weight * volume_far * kernel, axis=-1))
    relative = lax.optimization_barrier(jnp.sum((partner[:, :, 5:8, None, :] - center[:, :, 5:8, :, None]) * separation, axis=2))
    divergence = lax.optimization_barrier(jnp.sum(weight * volume_far * slope * relative, axis=-1))
    return jnp.stack([summed_mass, summed_volume, divergence], axis=2)

def force_terms(center, partner, shift):
    separation, kernel, slope = pair_geometry(center, partner, shift)
    weight = partner[:, :, 3, None, :]
    mass_far = partner[:, :, 4, None, :]
    dens_own = center[:, :, 9, :, None]
    dens_far = partner[:, :, 9, None, :]
    specific_own = center[:, :, 10, :, None] / (dens_own * dens_own)
    specific_far = partner[:, :, 10, None, :] / (dens_far * dens_far)
    visc_own = jnp.maximum(-center[:, :, 11, :, None], 0.0)
    visc_far = jnp.maximum(-partner[:, :, 11, None, :], 0.0)
    damping = 2.0 * (visc_own + visc_far) / (dens_own + dens_far)
    scaled = weight * mass_far * slope
    push = scaled * (specific_own + specific_far + damping)
    accel = -lax.optimization_barrier(jnp.sum(push[:, :, None] * separation, axis=-1))
    closing = lax.optimization_barrier(jnp.sum((center[:, :, 5:8, :, None] - partner[:, :, 5:8, None, :]) * separation, axis=2))
    heating = lax.optimization_barrier(jnp.sum(scaled * (specific_own + 0.5 * damping) * closing, axis=-1))
    return jnp.concatenate([accel, heating[:, :, None, :]], axis=2)

def sweep(padded, mask, terms_fn, width_out):
    rows = padded.shape[0] - 2
    cols = padded.shape[1] - 2
    depth = padded.shape[2] - 2
    chans = padded.shape[3]
    slots = padded.shape[4]
    zero = jnp.zeros((), jnp.int32)

    def leaf_row(index):
        slab = lax.dynamic_slice_in_dim(padded, index, 3, 0)
        center = slab[1, 1:-1, 1:-1]
        row_mask = None
        if mask is not None:
            row_mask = lax.dynamic_index_in_dim(mask, index, 0, keepdims=False).astype(jnp.float32)

        def partner_step(partner, total):
            off_x = partner // 9
            off_y = partner // 3 % 3
            off_z = partner % 3
            neighbour = lax.dynamic_slice(slab, (off_x, off_y, off_z, zero, zero), (1, cols, depth, chans, slots))[0]
            shift = jnp.stack([off_x, off_y, off_z]).astype(jnp.float32) - 1.0
            terms = terms_fn(center, neighbour, shift)
            if row_mask is not None:
                picked = lax.dynamic_index_in_dim(row_mask, partner, 2, keepdims=False)
                terms = terms * picked[:, :, None, None]
            return total + terms
        start = jnp.zeros((cols, depth, width_out, slots), jnp.float32)
        return lax.fori_loop(jnp.int32(0), jnp.int32(27), partner_step, start)
    return lax.map(leaf_row, jnp.arange(rows, dtype=jnp.int32))

def wrapped(field):
    return jnp.pad(field, ((1, 1), (1, 1), (1, 1), (0, 0), (0, 0)), mode='wrap')

def reference(offsets, velocity, mass, energy, partner_mask, counts):
    slot_ids = jnp.arange(P_SIZE, dtype=jnp.int32)
    valid = (slot_ids[None, None, None, :] < counts[:, :, :, None]).astype(jnp.float32)
    base = jnp.concatenate([offsets, valid[:, :, :, None], mass[:, :, :, None], velocity], axis=3)
    volume = 1.0 / (1.0 + sweep(wrapped(base[:, :, :, 0:4]), None, volume_terms, 1)[:, :, :, 0])
    second = jnp.concatenate([base, volume[:, :, :, None]], axis=3)
    summed = sweep(wrapped(second), partner_mask, density_terms, 3)
    density = (mass + summed[:, :, :, 0]) / (volume + summed[:, :, :, 1])
    divergence = summed[:, :, :, 2]
    pressure = 2.0 / 3.0 * density * energy
    state = jnp.stack([density, pressure, divergence], axis=3)
    third = jnp.concatenate([second, state], axis=3)
    forces = sweep(wrapped(third), partner_mask, force_terms, 4)
    acceleration = forces[:, :, :, 0:3] * valid[:, :, :, None]
    energy_rate = forces[:, :, :, 3] * valid
    return (acceleration, energy_rate)
```

```python
import jax
import jax.numpy as jnp
from jax import lax
from jax.experimental import pallas as pl
from jax.experimental.pallas import tpu as pltpu
from jax.sharding import PartitionSpec as P

F32 = jnp.float32
MESH = pl.DeviceIdType.MESH
AXES = ("gx", "gy", "gz")
CHUNK = 32
FAR = 1.0e3
DIRECTIONS = [
    (dx, dy, dz)
    for dx in (-1, 0, 1)
    for dy in (-1, 0, 1)
    for dz in (-1, 0, 1)
    if (dx, dy, dz) != (0, 0, 0)
]
LEAVES = [(ix, iy, iz) for ix in range(2) for iy in range(2) for iz in range(2)]
DIGITS = [(a, b, c) for a in range(3) for b in range(3) for c in range(3)]
INSIDE = [d for d in DIGITS if max(d) < 2]
OUTSIDE = [d for d in DIGITS if max(d) == 2]


def own_span(step):
    return {1: pl.ds(2, 1), -1: pl.ds(1, 1), 0: pl.ds(1, 2)}[step]


def halo_span(step):
    return {1: pl.ds(0, 1), -1: pl.ds(3, 1), 0: pl.ds(1, 2)}[step]


def neighbours():
    found = []
    for direction in DIRECTIONS:
        found.append(
            tuple(
                lax.rem(lax.axis_index(axis) + (step + lax.axis_size(axis)), lax.axis_size(axis))
                for axis, step in zip(AXES, direction)
            )
        )
    return found


def exchange(field, devices, send_sems, recv_sems):
    copies = []
    for index, direction in enumerate(DIRECTIONS):
        source = tuple(own_span(step) for step in direction)
        target = tuple(halo_span(step) for step in direction)
        copies.append(
            pltpu.make_async_remote_copy(
                src_ref=field.at[source],
                dst_ref=field.at[target],
                send_sem=send_sems.at[index],
                recv_sem=recv_sems.at[index],
                device_id=devices[index],
                device_id_type=MESH,
            )
        )
    for copy in copies:
        copy.start()
    return copies


def partner_of(leaf, digits):
    place = tuple(1 + d if d < 2 else 3 * i for i, d in zip(leaf, digits))
    offset = tuple(j - 1 - i for j, i in zip(place, leaf))
    number = 9 * (offset[0] + 1) + 3 * (offset[1] + 1) + offset[2] + 1
    return place, offset, number


def leaf_at(index):
    return (index // 4, (index // 2) % 2, index % 2)


def kernel(
    offsets_ref,
    velocity_ref,
    mass_ref,
    energy_ref,
    mask_ref,
    counts_ref,
    accel_ref,
    rate_ref,
    base,
    ratio,
    state,
    own,
    columns,
    far_columns,
    sums,
    mass_w,
    mass_g,
    mass_e,
    table,
    send_sems,
    recv_sems,
):
    devices = neighbours()
    barrier = pltpu.get_barrier_semaphore()
    for device in devices:
        pl.semaphore_signal(barrier, inc=1, device_id=device, device_id_type=MESH)

    slot = lax.broadcasted_iota(jnp.int32, (1, 128), 1)
    own[...] = jnp.zeros_like(own)
    for number, (ix, iy, iz) in enumerate(LEAVES):
        valid = slot < counts_ref[ix, iy, iz]
        place = (1 + ix, 1 + iy, 1 + iz)
        for d in range(3):
            spot = jnp.where(valid, 2.0 * offsets_ref[ix, iy, iz, d : d + 1, :], FAR)
            speed = velocity_ref[ix, iy, iz, d : d + 1, :]
            base[place + (slice(d, d + 1),)] = spot
            base[place + (slice(4 + d, 5 + d),)] = speed
            own[8 * d + number : 8 * d + number + 1, :] = spot
            own[8 * (3 + d) + number : 8 * (3 + d) + number + 1, :] = speed
        weight = mass_ref[ix, iy, iz : iz + 1, :]
        base[place + (slice(3, 4),)] = weight
        base[place + (slice(7, 8),)] = weight
        own[48 + number : 49 + number, :] = weight
        own[56 + number : 57 + number, :] = energy_ref[ix, iy, iz : iz + 1, :]
        own[64 + number : 65 + number, :] = valid.astype(F32)

    copies = []
    pl.semaphore_wait(barrier, len(DIRECTIONS))
    first = exchange(base, devices, send_sems.at[0], recv_sems.at[0])
    copies += first

    turned = jnp.transpose(own[...])
    for f in range(6):
        for number in range(8):
            column = 8 * f + number
            columns[f, number] = jnp.broadcast_to(turned[:, column : column + 1], (128, 128))

    def over_chunks(body):
        def step(n, carry):
            body(n // (128 // CHUNK), (n % (128 // CHUNK)) * CHUNK)
            return carry

        lax.fori_loop(0, 8 * (128 // CHUNK), step, 0)

    def first_pass(digit_list, fresh):
        def body(number, start):
            leaf = leaf_at(number)
            rows = pl.ds(pl.multiple_of(start, CHUNK), CHUNK)
            if fresh:
                volume = jnp.zeros((CHUNK, 128), F32)
                weighed = jnp.zeros((CHUNK, 128), F32)
            else:
                volume = sums[0, number, rows, :]
                weighed = sums[1, number, rows, :]
            for digits in digit_list:
                place, offset, k = partner_of(leaf, digits)
                picked = mask_ref[leaf + (k,)].astype(F32)
                square = None
                closing = None
                for d in range(3):
                    far = base[place + (slice(d, d + 1),)] + 2.0 * offset[d].astype(F32)
                    gap = columns[d, number, rows, :] - far
                    rush = base[place + (slice(4 + d, 5 + d),)] - columns[3 + d, number, rows, :]
                    square = gap * gap if square is None else square + gap * gap
                    closing = rush * gap if closing is None else closing + rush * gap
                square = jnp.maximum(square, 1.0e-30)
                inside = jnp.maximum(2.0 - square * lax.rsqrt(square), 0.0)
                two = inside * inside
                weight = base[place + (slice(3, 4),)] * picked
                smooth = two * two * (2.5 - inside)
                volume = volume + smooth
                smooth = smooth * weight
                weighed = weighed + smooth
                slope = two * inside * weight
                mass_w[number, k, rows, :] = smooth
                mass_g[number, k, rows, :] = slope
                mass_e[number, k, rows, :] = slope * closing
            sums[0, number, rows, :] = volume
            sums[1, number, rows, :] = weighed

        over_chunks(body)

    def second_pass(digit_list, fresh):
        def body(number, start):
            leaf = leaf_at(number)
            rows = pl.ds(pl.multiple_of(start, CHUNK), CHUNK)
            if fresh:
                volume = jnp.zeros((CHUNK, 128), F32)
                spread = jnp.zeros((CHUNK, 128), F32)
            else:
                volume = sums[2, number, rows, :]
                spread = sums[3, number, rows, :]
            for digits in digit_list:
                place, offset, k = partner_of(leaf, digits)
                weight = ratio[place + (slice(0, 1),)]
                volume = volume + weight * mass_w[number, k, rows, :]
                spread = spread + weight * mass_e[number, k, rows, :]
            sums[2, number, rows, :] = volume
            sums[3, number, rows, :] = spread

        over_chunks(body)

    def third_pass(digit_list, fresh):
        def body(number, start):
            leaf = leaf_at(number)
            rows = pl.ds(pl.multiple_of(start, CHUNK), CHUNK)
            if fresh:
                totals = [jnp.zeros((CHUNK, 128), F32)] * 5
            else:
                totals = [sums[f, number, rows, :] for f in range(5)]
            for digits in digit_list:
                place, offset, k = partner_of(leaf, digits)
                dense = far_columns[0, number, rows, :] + state[place + (slice(0, 1),)]
                sticky = far_columns[1, number, rows, :] + state[place + (slice(1, 2),)]
                damp = sticky * pltpu.reciprocal(dense, approx=True)
                mine = far_columns[2, number, rows, :] + damp
                theirs = state[place + (slice(2, 3),)] + damp
                push = mass_g[number, k, rows, :] * (mine + theirs)
                totals[0] = totals[0] + push
                for d in range(3):
                    far = base[place + (slice(d, d + 1),)] + 2.0 * offset[d].astype(F32)
                    totals[1 + d] = totals[1 + d] + push * far
                totals[4] = totals[4] + mass_e[number, k, rows, :] * mine
            for f in range(5):
                sums[f, number, rows, :] = totals[f]

        over_chunks(body)

    lane = lax.broadcasted_iota(jnp.int32, (128, 128), 1)

    def gathered(fields):
        packed = jnp.zeros((128, 128), F32)
        for f in fields:
            for number in range(8):
                total = jnp.sum(sums[f, number], axis=1, keepdims=True)
                packed = jnp.where(lane == 8 * f + number, total, packed)
        table[...] = jnp.transpose(packed)

    first_pass(INSIDE, True)
    for copy in first:
        copy.wait_recv()
    first_pass(OUTSIDE, False)

    gathered((0, 1))
    mass = own[48:56, :]
    volume = 1.0 / (1.0 + 0.125 * table[0:8, :])
    summed_mass = mass + 0.125 * table[8:16, :]
    rated = volume / mass
    for number, (ix, iy, iz) in enumerate(LEAVES):
        ratio[1 + ix, 1 + iy, 1 + iz] = rated[number : number + 1, :]
    second = exchange(ratio, devices, send_sems.at[1], recv_sems.at[1])
    copies += second
    second_pass(INSIDE, True)
    for copy in second:
        copy.wait_recv()
    second_pass(OUTSIDE, False)

    gathered((2, 3))
    density = summed_mass / (volume + 0.125 * table[16:24, :])
    sticky = jnp.maximum(1.25 * table[24:32, :], 0.0)
    specific = (2.0 / 3.0) * own[56:64, :] / density
    for number, (ix, iy, iz) in enumerate(LEAVES):
        place = (1 + ix, 1 + iy, 1 + iz)
        for f, rows in enumerate((density, sticky, specific)):
            state[place + (slice(f, f + 1),)] = rows[number : number + 1, :]
        state[place + (slice(3, 4),)] = jnp.zeros((1, 128), F32)
    third = exchange(state, devices, send_sems.at[2], recv_sems.at[2])
    copies += third
    own[0:8, :] = density
    own[8:16, :] = sticky
    own[16:24, :] = specific
    turned = jnp.transpose(own[...])
    for f in range(3):
        for number in range(8):
            column = 8 * f + number
            far_columns[f, number] = jnp.broadcast_to(turned[:, column : column + 1], (128, 128))
    third_pass(INSIDE, True)
    for copy in third:
        copy.wait_recv()
    third_pass(OUTSIDE, False)

    gathered((0, 1, 2, 3, 4))
    for number, (ix, iy, iz) in enumerate(LEAVES):
        valid = own[64 + number : 65 + number, :] > 0.5
        total = table[number : number + 1, :]
        for d in range(3):
            row = 8 * (1 + d) + number
            spot = base[1 + ix, 1 + iy, 1 + iz, d : d + 1, :]
            value = 1.25 * (spot * total - table[row : row + 1, :])
            accel_ref[ix, iy, iz, d : d + 1, :] = jnp.where(valid, value, 0.0)
        rate_ref[ix, iy, iz : iz + 1, :] = jnp.where(
            valid, 1.25 * table[32 + number : 33 + number, :], 0.0
        )
    for copy in copies:
        copy.wait_send()


def shards(offsets, velocity, mass, energy, partner_mask, counts):
    vmem = pl.BlockSpec(memory_space=pltpu.VMEM)
    smem = pl.BlockSpec(memory_space=pltpu.SMEM)
    return pl.pallas_call(
        kernel,
        out_shape=(
            jax.ShapeDtypeStruct(offsets.shape, F32),
            jax.ShapeDtypeStruct(mass.shape, F32),
        ),
        in_specs=[vmem] * 4 + [smem] * 2,
        out_specs=(vmem, vmem),
        scratch_shapes=[
            pltpu.VMEM((4, 4, 4, 8, 128), F32),
            pltpu.VMEM((4, 4, 4, 1, 128), F32),
            pltpu.VMEM((4, 4, 4, 4, 128), F32),
            pltpu.VMEM((128, 128), F32),
            pltpu.VMEM((6, 8, 128, 128), F32),
            pltpu.VMEM((3, 8, 128, 128), F32),
            pltpu.VMEM((5, 8, 128, 128), F32),
            pltpu.VMEM((8, 27, 128, 128), F32),
            pltpu.VMEM((8, 27, 128, 128), F32),
            pltpu.VMEM((8, 27, 128, 128), F32),
            pltpu.VMEM((128, 128), F32),
            pltpu.SemaphoreType.DMA((3, 26)),
            pltpu.SemaphoreType.DMA((3, 26)),
        ],
        compiler_params=pltpu.CompilerParams(
            collective_id=0,
            has_side_effects=True,
            vmem_limit_bytes=60 * 1024 * 1024,
        ),
    )(offsets, velocity, mass, energy, partner_mask, counts)


def solution(mesh):
    placed = (
        P("gx", "gy", "gz", None, None),
        P("gx", "gy", "gz", None, None),
        P("gx", "gy", "gz", None),
        P("gx", "gy", "gz", None),
        P("gx", "gy", "gz", None),
        P("gx", "gy", "gz"),
    )
    return jax.shard_map(
        shards,
        mesh=mesh,
        in_specs=placed,
        out_specs=(P("gx", "gy", "gz", None, None), P("gx", "gy", "gz", None)),
        check_vma=False,
    )
```

```python
import jax
import jax.numpy as jnp
from jax import lax
from jax.experimental import pallas as pl
from jax.experimental.pallas import tpu as pltpu
from jax.sharding import PartitionSpec as P

F32 = jnp.float32
BF16 = jnp.bfloat16
MESH = pl.DeviceIdType.MESH
AXES = ("gx", "gy", "gz")
FAR = 1.0e2
DEPTH = 80
DIRECTIONS = [
    (dx, dy, dz)
    for dz in (1, 0, -1)
    for dx in (-1, 0, 1)
    for dy in (-1, 0, 1)
    if (dx, dy, dz) != (0, 0, 0)
]
UPWARD = 9
EVERY = range(len(DIRECTIONS))
LEAVES = [(ix, iy, iz) for ix in range(2) for iy in range(2) for iz in range(2)]
DIGITS = [(a, b, c) for a in range(3) for b in range(3) for c in range(3)]
INSIDE = [d for d in DIGITS if max(d) < 2]
BESIDE = [d for d in DIGITS if max(d) == 2 and d[2] < 2]
BEYOND = [d for d in DIGITS if d[2] == 2]


def own_span(step):
    return {1: pl.ds(2, 1), -1: pl.ds(1, 1), 0: pl.ds(1, 2)}[step]


def halo_span(step):
    return {1: pl.ds(0, 1), -1: pl.ds(3, 1), 0: pl.ds(1, 2)}[step]


def neighbours():
    found = []
    for direction in DIRECTIONS:
        found.append(
            tuple(
                lax.rem(lax.axis_index(axis) + (step + lax.axis_size(axis)), lax.axis_size(axis))
                for axis, step in zip(AXES, direction)
            )
        )
    return found


def exchange(field, devices, send_sems, recv_sems, indices):
    copies = []
    for index in indices:
        direction = DIRECTIONS[index]
        copies.append(
            pltpu.make_async_remote_copy(
                src_ref=field.at[tuple(own_span(step) for step in direction)],
                dst_ref=field.at[tuple(halo_span(step) for step in direction)],
                send_sem=send_sems.at[index],
                recv_sem=recv_sems.at[index],
                device_id=devices[index],
                device_id_type=MESH,
            )
        )
    for copy in copies:
        copy.start()
    return copies


def partners(leaf, digit_list):
    places, steps = [], []
    for axis, i in enumerate(leaf):
        places.append((1, 2, 3 * i))
        steps.append([3 ** (2 - axis) * (j - i) for j in places[-1]])
    for digits in digit_list:
        yield (
            tuple(places[axis][d] for axis, d in enumerate(digits)),
            sum(steps[axis][d] for axis, d in enumerate(digits)),
            DIGITS.index(digits),
        )


def kernel(
    offsets_ref,
    velocity_ref,
    mass_ref,
    energy_ref,
    mask_ref,
    counts_ref,
    accel_ref,
    rate_ref,
    base,
    placed,
    ratio,
    state,
    own,
    near_terms,
    far_terms,
    far_columns,
    sums,
    mass_w,
    mass_g,
    mass_e,
    pack,
    table,
    send_sems,
    recv_sems,
):
    devices = neighbours()
    barrier = pltpu.get_barrier_semaphore()
    for device in devices:
        pl.semaphore_signal(barrier, inc=1, device_id=device, device_id_type=MESH)

    slot = lax.broadcasted_iota(jnp.int32, (1, 128), 1)
    own[...] = jnp.zeros_like(own)
    for number, (ix, iy, iz) in enumerate(LEAVES):
        valid = slot < counts_ref[ix, iy, iz]
        place = (1 + ix, 1 + iy, 1 + iz)
        for d in range(3):
            spot = jnp.where(valid, 2.0 * offsets_ref[ix, iy, d, iz : iz + 1, :], FAR)
            base[place + (slice(d, d + 1),)] = spot
            base[place + (slice(4 + d, 5 + d),)] = velocity_ref[ix, iy, d, iz : iz + 1, :]
        weight = mass_ref[ix, iy, iz : iz + 1, :]
        base[place + (slice(3, 4),)] = weight
        base[place + (slice(7, 8),)] = weight
        own[48 + number : 49 + number, :] = weight
        own[56 + number : 57 + number, :] = energy_ref[ix, iy, iz : iz + 1, :]
        own[64 + number : 65 + number, :] = valid.astype(F32)

    pl.semaphore_wait(barrier, len(DIRECTIONS))
    first = exchange(base, devices, send_sems.at[0], recv_sems.at[0], EVERY)

    line = lax.broadcasted_iota(jnp.int32, (8, 128), 0)

    def marked(*chosen):
        found = line == chosen[0]
        for row in chosen[1:]:
            found = found | (line == row)
        return found.astype(F32)

    axes = [marked(d) for d in range(3)]
    positions = marked(0, 1, 2)
    both = marked(0, 1, 2, 4, 5, 6)
    one, last = marked(3), marked(7)
    nothing = jnp.zeros((8, 128), F32)

    def framed(place):
        shift = sum(axes[d] * jnp.float32(2 * (place[d] - 2)) for d in range(3))
        return base[place] + shift

    def split(rows):
        high = rows.astype(BF16).astype(F32)
        rest = rows - high
        middle = rest.astype(BF16).astype(F32)
        return high, middle, rest - middle

    def make_far(place):
        rows = framed(place)
        placed[place] = rows
        swapped = pltpu.roll(rows, 4, 0)
        halves = []
        for linear, product in (
            (rows * (-2.0 * positions) + one, rows * rows),
            (swapped * both - last, -(rows * swapped)),
        ):
            high, middle, low = split(linear)
            parts = [high, high, high, middle, middle, low, *split(product), nothing]
            halves.append(jnp.concatenate(parts, axis=0))
        far_terms[place] = jnp.concatenate(halves, axis=1).astype(BF16)

    def make_near(number, place):
        rows = framed(place)
        swapped = pltpu.roll(rows, 4, 0)
        square = jnp.sum(rows * rows * positions, axis=0, keepdims=True)
        along = jnp.sum(rows * swapped * positions, axis=0, keepdims=True)
        rows = rows * both + one * square + last * along
        high, middle, low = split(rows)
        parts = [high, middle, low, high, middle, high, positions, positions, positions]
        parts += [nothing] * 7
        near_terms[number] = jnp.transpose(jnp.concatenate(parts, axis=0))[:, 0:DEPTH].astype(BF16)

    for number, (ix, iy, iz) in enumerate(LEAVES):
        make_near(number, (1 + ix, 1 + iy, 1 + iz))
        make_far((1 + ix, 1 + iy, 1 + iz))

    def make_outer_far(levels):
        for place in [(x, y, z) for x in range(4) for y in range(4) for z in levels]:
            if any(j in (0, 3) for j in place):
                make_far(place)

    def over_columns(body):
        def step(n, carry):
            body(n // 2, n % 2)
            return carry

        lax.fori_loop(0, 4, step, 0)

    def first_pass(shared, work, fresh=False):
        def body(ix, iy):
            numbers = [4 * ix + 2 * iy + level for level in range(2)]
            if fresh:
                totals = [[jnp.zeros((128, 128), F32)] * 2] * 2
            else:
                totals = [[sums[f, number] for f in range(2)] for number in numbers]

            def add(level, place, k, entry, product):
                number = numbers[level]
                volume, weighed = totals[level]
                square = jnp.maximum(product[:, 0:128], 1.0e-30)
                inside = jnp.maximum(2.0 - square * lax.rsqrt(square), 0.0)
                two = inside * inside
                picked = mask_ref[ix, iy, level, k].astype(F32)
                weight = base[place + (slice(3, 4),)] * picked
                smooth = two * two * (2.5 - inside)
                volume = volume + smooth
                smooth = smooth * weight
                weighed = weighed + smooth
                slope = two * inside * weight
                mass_w[number, entry] = smooth
                mass_g[number, entry] = slope
                mass_e[number, entry] = slope * product[:, 128:256]
                totals[level] = [volume, weighed]

            pair = near_terms[pl.ds(numbers[0], 2)].reshape(256, DEPTH)
            for low, high in zip(*(partners((ix, iy, level), shared) for level in range(2))):
                product = jnp.dot(pair, far_terms[low[0]], preferred_element_type=F32)
                add(0, *low, product[0:128])
                add(1, *high, product[128:256])
            for level, digit_list in work:
                for place, k, entry in partners((ix, iy, level), digit_list):
                    near = near_terms[numbers[level]]
                    product = jnp.dot(near, far_terms[place], preferred_element_type=F32)
                    add(level, place, k, entry, product)
            for level in range(2):
                for f in range(2):
                    sums[f, numbers[level]] = totals[level][f]

        over_columns(body)

    def second_pass(work, fresh=False):
        def body(ix, iy):
            for level, digit_list in work:
                leaf = (ix, iy, level)
                number = 4 * ix + 2 * iy + level
                if fresh:
                    volume = jnp.zeros((128, 128), F32)
                    spread = jnp.zeros((128, 128), F32)
                else:
                    volume = sums[2, number]
                    spread = sums[3, number]
                for place, k, entry in partners(leaf, digit_list):
                    weight = ratio[place + (slice(0, 1),)]
                    volume = volume + weight * mass_w[number, entry]
                    spread = spread + weight * mass_e[number, entry]
                sums[2, number] = volume
                sums[3, number] = spread

        over_columns(body)

    def third_pass(work, fresh=False):
        def body(ix, iy):
            for level, digit_list in work:
                leaf = (ix, iy, level)
                number = 4 * ix + 2 * iy + level
                if fresh:
                    totals = [jnp.zeros((128, 128), F32)] * 5
                else:
                    totals = [sums[f, number] for f in range(5)]
                for place, k, entry in partners(leaf, digit_list):
                    dense = far_columns[0, number] + state[place + (slice(0, 1),)]
                    sticky = far_columns[1, number] + state[place + (slice(1, 2),)]
                    damp = sticky * pltpu.reciprocal(dense, approx=True)
                    mine = far_columns[2, number] + damp
                    theirs = state[place + (slice(2, 3),)] + damp
                    push = mass_g[number, entry] * (mine + theirs)
                    totals[0] = totals[0] + push
                    for d in range(3):
                        totals[1 + d] = totals[1 + d] + push * placed[place + (slice(d, d + 1),)]
                    totals[4] = totals[4] + mass_e[number, entry] * mine
                for f in range(5):
                    sums[f, number] = totals[f]

        over_columns(body)

    lane = lax.broadcasted_iota(jnp.int32, (128, 128), 1)

    def gather(fields, numbers, fresh=False):
        packed = jnp.zeros((128, 128), F32) if fresh else pack[...]
        for f in fields:
            for number in numbers:
                total = jnp.sum(sums[f, number], axis=1, keepdims=True)
                packed = jnp.where(lane == 8 * f + number, total, packed)
        pack[...] = packed

    lower, upper = range(0, 8, 2), range(1, 8, 2)

    first_pass(INSIDE, [], fresh=True)
    for copy in first[UPWARD:]:
        copy.wait_recv()
    make_outer_far((1, 2, 3))
    first_pass(BESIDE, [(1, BEYOND)])
    for copy in first[:UPWARD]:
        copy.wait_recv()
    make_outer_far((0,))
    first_pass([], [(0, BEYOND)])

    gather((0, 1), range(8), fresh=True)
    table[...] = jnp.transpose(pack[...])
    mass = own[48:56, :]
    volume = 1.0 / (1.0 + 0.125 * table[0:8, :])
    summed_mass = mass + 0.125 * table[8:16, :]
    rated = volume / mass
    for number, (ix, iy, iz) in enumerate(LEAVES):
        ratio[1 + ix, 1 + iy, 1 + iz] = rated[number : number + 1, :]
    second = exchange(ratio, devices, send_sems.at[1], recv_sems.at[1], EVERY)

    def finish_state(numbers):
        gather((2, 3), numbers)
        table[...] = jnp.transpose(pack[...])
        density = summed_mass / (volume + 0.125 * table[16:24, :])
        sticky = jnp.maximum(1.25 * table[24:32, :], 0.0)
        specific = (2.0 / 3.0) * own[56:64, :] / density
        for number in numbers:
            place = tuple(1 + i for i in LEAVES[number])
            for f, rows in enumerate((density, sticky, specific)):
                row = rows[number : number + 1, :]
                state[place + (slice(f, f + 1),)] = row
                own[8 * f + number : 8 * f + number + 1, :] = row
            state[place + (slice(3, 4),)] = jnp.zeros((1, 128), F32)

    second_pass([(0, INSIDE), (1, INSIDE)], fresh=True)
    for copy in second[UPWARD:]:
        copy.wait_recv()
    second_pass([(0, BESIDE), (1, BESIDE + BEYOND)])
    finish_state(upper)
    third = exchange(state, devices, send_sems.at[2], recv_sems.at[2], EVERY[:UPWARD])
    for copy in second[:UPWARD]:
        copy.wait_recv()
    second_pass([(0, BEYOND)])
    finish_state(lower)
    third += exchange(state, devices, send_sems.at[2], recv_sems.at[2], EVERY[UPWARD:])

    turned = jnp.transpose(own[...])
    for f in range(3):
        for number in range(8):
            column = 8 * f + number
            far_columns[f, number] = jnp.broadcast_to(turned[:, column : column + 1], (128, 128))

    third_pass([(0, INSIDE), (1, INSIDE)], fresh=True)
    for copy in third[UPWARD:]:
        copy.wait_recv()
    third_pass([(0, BESIDE), (1, BESIDE + BEYOND)])
    gather(range(5), upper, fresh=True)
    for copy in third[:UPWARD]:
        copy.wait_recv()
    third_pass([(0, BEYOND)])
    gather(range(5), lower)
    table[...] = jnp.transpose(pack[...])

    for number, (ix, iy, iz) in enumerate(LEAVES):
        valid = own[64 + number : 65 + number, :] > 0.5
        total = table[number : number + 1, :]
        for d in range(3):
            row = 8 * (1 + d) + number
            spot = placed[1 + ix, 1 + iy, 1 + iz, d : d + 1, :]
            value = 1.25 * (spot * total - table[row : row + 1, :])
            accel_ref[ix, iy, d, iz : iz + 1, :] = jnp.where(valid, value, 0.0)
        rate_ref[ix, iy, iz : iz + 1, :] = jnp.where(
            valid, 1.25 * table[32 + number : 33 + number, :], 0.0
        )
    for copy in first + second + third:
        copy.wait_send()


def shards(offsets, velocity, mass, energy, partner_mask, counts):
    vmem = pl.BlockSpec(memory_space=pltpu.VMEM)
    smem = pl.BlockSpec(memory_space=pltpu.SMEM)
    offsets = jnp.transpose(offsets, (0, 1, 3, 2, 4))
    velocity = jnp.transpose(velocity, (0, 1, 3, 2, 4))
    acceleration, rate = pl.pallas_call(
        kernel,
        out_shape=(
            jax.ShapeDtypeStruct(offsets.shape, F32),
            jax.ShapeDtypeStruct(mass.shape, F32),
        ),
        in_specs=[vmem] * 4 + [smem] * 2,
        out_specs=(vmem, vmem),
        scratch_shapes=[
            pltpu.VMEM((4, 4, 4, 8, 128), F32),
            pltpu.VMEM((4, 4, 4, 8, 128), F32),
            pltpu.VMEM((4, 4, 4, 1, 128), F32),
            pltpu.VMEM((4, 4, 4, 4, 128), F32),
            pltpu.VMEM((128, 128), F32),
            pltpu.VMEM((8, 128, DEPTH), BF16),
            pltpu.VMEM((4, 4, 4, DEPTH, 256), BF16),
            pltpu.VMEM((3, 8, 128, 128), F32),
            pltpu.VMEM((5, 8, 128, 128), F32),
            pltpu.VMEM((8, 27, 128, 128), F32),
            pltpu.VMEM((8, 27, 128, 128), F32),
            pltpu.VMEM((8, 27, 128, 128), F32),
            pltpu.VMEM((128, 128), F32),
            pltpu.VMEM((128, 128), F32),
            pltpu.SemaphoreType.DMA((3, 26)),
            pltpu.SemaphoreType.DMA((3, 26)),
        ],
        compiler_params=pltpu.CompilerParams(
            collective_id=0,
            has_side_effects=True,
            vmem_limit_bytes=60 * 1024 * 1024,
        ),
    )(offsets, velocity, mass, energy, partner_mask, counts)
    return jnp.transpose(acceleration, (0, 1, 3, 2, 4)), rate


def solution(mesh):
    placed = (
        P("gx", "gy", "gz", None, None),
        P("gx", "gy", "gz", None, None),
        P("gx", "gy", "gz", None),
        P("gx", "gy", "gz", None),
        P("gx", "gy", "gz", None),
        P("gx", "gy", "gz"),
    )
    return jax.shard_map(
        shards,
        mesh=mesh,
        in_specs=placed,
        out_specs=(P("gx", "gy", "gz", None, None), P("gx", "gy", "gz", None)),
        check_vma=False,
    )
```

```python
import jax
import jax.numpy as jnp
from jax import lax
from jax.experimental import pallas as pl
from jax.experimental.pallas import tpu as pltpu
from jax.sharding import PartitionSpec as P

F32 = jnp.float32
BF16 = jnp.bfloat16
MESH = pl.DeviceIdType.MESH
AXES = ("gx", "gy", "gz")
FAR = 1.0e2
DEPTH = 80
DIRECTIONS = [
    (dx, dy, dz)
    for dz in (1, 0, -1)
    for dx in (-1, 0, 1)
    for dy in (-1, 0, 1)
    if (dx, dy, dz) != (0, 0, 0)
]
UPWARD = 9
EVERY = sorted(range(len(DIRECTIONS)), key=lambda i: -abs(DIRECTIONS[i][0]) - abs(DIRECTIONS[i][1]))
LEAVES = [(ix, iy, iz) for ix in range(2) for iy in range(2) for iz in range(2)]
DIGITS = [(a, b, c) for a in range(3) for b in range(3) for c in range(3)]
INSIDE = [d for d in DIGITS if max(d) < 2]
BESIDE = [d for d in DIGITS if max(d) == 2 and d[2] < 2]
BEYOND = [d for d in DIGITS if d[2] == 2]


def own_span(step):
    return {1: pl.ds(2, 1), -1: pl.ds(1, 1), 0: pl.ds(1, 2)}[step]


def halo_span(step):
    return {1: pl.ds(0, 1), -1: pl.ds(3, 1), 0: pl.ds(1, 2)}[step]


def neighbours():
    found = []
    for direction in DIRECTIONS:
        found.append(
            tuple(
                lax.rem(lax.axis_index(axis) + (step + lax.axis_size(axis)), lax.axis_size(axis))
                for axis, step in zip(AXES, direction)
            )
        )
    return found


def exchange(field, devices, send_sem, recv_sems, indices):
    for index in indices:
        direction = DIRECTIONS[index]
        pltpu.make_async_remote_copy(
            src_ref=field.at[tuple(own_span(step) for step in direction)],
            dst_ref=field.at[tuple(halo_span(step) for step in direction)],
            send_sem=send_sem,
            recv_sem=recv_sems.at[0 if index < UPWARD else 1],
            device_id=devices[index],
            device_id_type=MESH,
        ).start()


def await_leaves(count, like, semaphore):
    block = like.at[pl.ds(0, count)]
    pltpu.make_async_copy(block, block, semaphore).wait()


def partners(leaf, digit_list):
    places, steps = [], []
    for axis, i in enumerate(leaf):
        places.append((1, 2, 3 * i))
        steps.append([3 ** (2 - axis) * (j - i) for j in places[-1]])
    for digits in digit_list:
        yield (
            tuple(places[axis][d] for axis, d in enumerate(digits)),
            sum(steps[axis][d] for axis, d in enumerate(digits)),
            DIGITS.index(digits),
        )


def kernel(
    offsets_ref,
    velocity_ref,
    mass_ref,
    energy_ref,
    mask_ref,
    counts_ref,
    accel_ref,
    rate_ref,
    base,
    placed,
    ratio,
    state,
    own,
    near_terms,
    far_terms,
    far_columns,
    sums,
    mass_w,
    mass_g,
    mass_e,
    pack,
    table,
    ghost_base,
    ghost_ratio,
    ghost_state,
    send_sems,
    recv_sems,
):
    devices = neighbours()
    barrier = pltpu.get_barrier_semaphore()
    for device in devices:
        pl.semaphore_signal(barrier, inc=1, device_id=device, device_id_type=MESH)

    slot = lax.broadcasted_iota(jnp.int32, (1, 128), 1)
    own[...] = jnp.zeros_like(own)
    for number, (ix, iy, iz) in enumerate(LEAVES):
        valid = slot < counts_ref[ix, iy, iz]
        place = (1 + ix, 1 + iy, 1 + iz)
        for d in range(3):
            spot = jnp.where(valid, 2.0 * offsets_ref[ix, iy, d, iz : iz + 1, :], FAR)
            base[place + (slice(d, d + 1),)] = spot
            base[place + (slice(4 + d, 5 + d),)] = velocity_ref[ix, iy, d, iz : iz + 1, :]
        weight = mass_ref[ix, iy, iz : iz + 1, :]
        base[place + (slice(3, 4),)] = weight
        base[place + (slice(7, 8),)] = weight
        own[48 + number : 49 + number, :] = weight
        own[56 + number : 57 + number, :] = energy_ref[ix, iy, iz : iz + 1, :]
        own[64 + number : 65 + number, :] = valid.astype(F32)

    pl.semaphore_wait(barrier, len(DIRECTIONS))
    exchange(base, devices, send_sems.at[0], recv_sems.at[0], EVERY)

    line = lax.broadcasted_iota(jnp.int32, (8, 128), 0)

    def marked(*chosen):
        found = line == chosen[0]
        for row in chosen[1:]:
            found = found | (line == row)
        return found.astype(F32)

    axes = [marked(d) for d in range(3)]
    positions = marked(0, 1, 2)
    both = marked(0, 1, 2, 4, 5, 6)
    one, last = marked(3), marked(7)
    nothing = jnp.zeros((8, 128), F32)

    def framed(place):
        shift = sum(axes[d] * jnp.float32(2 * (place[d] - 2)) for d in range(3))
        return base[place] + shift

    def split(rows):
        high = rows.astype(BF16).astype(F32)
        rest = rows - high
        middle = rest.astype(BF16).astype(F32)
        return high, middle, rest - middle

    def make_far(place):
        rows = framed(place)
        placed[place] = rows
        swapped = pltpu.roll(rows, 4, 0)
        halves = []
        for linear, product in (
            (rows * (-2.0 * positions) + one, rows * rows),
            (swapped * both - last, -(rows * swapped)),
        ):
            high, middle, low = split(linear)
            parts = [high, high, high, middle, middle, low, *split(product), nothing]
            halves.append(jnp.concatenate(parts, axis=0))
        far_terms[place] = jnp.concatenate(halves, axis=1).astype(BF16)

    def make_near(number, place):
        rows = framed(place)
        swapped = pltpu.roll(rows, 4, 0)
        square = jnp.sum(rows * rows * positions, axis=0, keepdims=True)
        along = jnp.sum(rows * swapped * positions, axis=0, keepdims=True)
        rows = rows * both + one * square + last * along
        high, middle, low = split(rows)
        parts = [high, middle, low, high, middle, high, positions, positions, positions]
        parts += [nothing] * 7
        near_terms[number] = jnp.transpose(jnp.concatenate(parts, axis=0))[:, 0:DEPTH].astype(BF16)

    for number, (ix, iy, iz) in enumerate(LEAVES):
        make_near(number, (1 + ix, 1 + iy, 1 + iz))
        make_far((1 + ix, 1 + iy, 1 + iz))

    def make_outer_far(levels):
        for place in [(x, y, z) for x in range(4) for y in range(4) for z in levels]:
            if any(j in (0, 3) for j in place):
                make_far(place)

    def over_columns(body):
        def step(n, carry):
            body(n // 2, n % 2)
            return carry

        lax.fori_loop(0, 4, step, 0)

    def first_pass(shared, work, fresh=False):
        def body(ix, iy):
            numbers = [4 * ix + 2 * iy + level for level in range(2)]
            if fresh:
                totals = [[jnp.zeros((128, 128), F32)] * 2] * 2
            else:
                totals = [[sums[f, number] for f in range(2)] for number in numbers]

            def add(level, place, k, entry, product):
                number = numbers[level]
                volume, weighed = totals[level]
                square = jnp.maximum(product[:, 0:128], 1.0e-30)
                inside = jnp.maximum(2.0 - square * lax.rsqrt(square), 0.0)
                two = inside * inside
                picked = mask_ref[ix, iy, level, k].astype(F32)
                weight = base[place + (slice(3, 4),)] * picked
                smooth = two * two * (2.5 - inside)
                volume = volume + smooth
                smooth = smooth * weight
                weighed = weighed + smooth
                slope = two * inside * weight
                mass_w[number, entry] = smooth
                mass_g[number, entry] = slope
                mass_e[number, entry] = slope * product[:, 128:256]
                totals[level] = [volume, weighed]

            pair = near_terms[pl.ds(numbers[0], 2)].reshape(256, DEPTH)
            for low, high in zip(*(partners((ix, iy, level), shared) for level in range(2))):
                product = jnp.dot(pair, far_terms[low[0]], preferred_element_type=F32)
                add(0, *low, product[0:128])
                add(1, *high, product[128:256])
            for level, digit_list in work:
                for place, k, entry in partners((ix, iy, level), digit_list):
                    near = near_terms[numbers[level]]
                    product = jnp.dot(near, far_terms[place], preferred_element_type=F32)
                    add(level, place, k, entry, product)
            for level in range(2):
                for f in range(2):
                    sums[f, numbers[level]] = totals[level][f]

        over_columns(body)

    def second_pass(work, fresh=False):
        def body(ix, iy):
            for level, digit_list in work:
                leaf = (ix, iy, level)
                number = 4 * ix + 2 * iy + level
                if fresh:
                    volume = jnp.zeros((128, 128), F32)
                    spread = jnp.zeros((128, 128), F32)
                else:
                    volume = sums[2, number]
                    spread = sums[3, number]
                for place, k, entry in partners(leaf, digit_list):
                    weight = ratio[place + (slice(0, 1),)]
                    volume = volume + weight * mass_w[number, entry]
                    spread = spread + weight * mass_e[number, entry]
                sums[2, number] = volume
                sums[3, number] = spread

        over_columns(body)

    def third_pass(work, fresh=False):
        def body(ix, iy):
            for level, digit_list in work:
                leaf = (ix, iy, level)
                number = 4 * ix + 2 * iy + level
                if fresh:
                    totals = [jnp.zeros((128, 128), F32)] * 5
                else:
                    totals = [sums[f, number] for f in range(5)]
                for place, k, entry in partners(leaf, digit_list):
                    dense = far_columns[0, number] + state[place + (slice(0, 1),)]
                    sticky = far_columns[1, number] + state[place + (slice(1, 2),)]
                    damp = sticky * pltpu.reciprocal(dense, approx=True)
                    mine = far_columns[2, number] + damp
                    theirs = state[place + (slice(2, 3),)] + damp
                    push = mass_g[number, entry] * (mine + theirs)
                    totals[0] = totals[0] + push
                    for d in range(3):
                        totals[1 + d] = totals[1 + d] + push * placed[place + (slice(d, d + 1),)]
                    totals[4] = totals[4] + mass_e[number, entry] * mine
                for f in range(5):
                    sums[f, number] = totals[f]

        over_columns(body)

    lane = lax.broadcasted_iota(jnp.int32, (128, 128), 1)

    def gather(fields, numbers, fresh=False):
        packed = jnp.zeros((128, 128), F32) if fresh else pack[...]
        for f in fields:
            for number in numbers:
                total = jnp.sum(sums[f, number], axis=1, keepdims=True)
                packed = jnp.where(lane == 8 * f + number, total, packed)
        pack[...] = packed

    lower, upper = range(0, 8, 2), range(1, 8, 2)

    first_pass(INSIDE, [], fresh=True)
    await_leaves(40, ghost_base, recv_sems.at[0, 1])
    make_outer_far((1, 2, 3))
    first_pass(BESIDE, [(1, BEYOND)])
    await_leaves(16, ghost_base, recv_sems.at[0, 0])
    make_outer_far((0,))
    first_pass([], [(0, BEYOND)])

    gather((0, 1), range(8), fresh=True)
    table[...] = jnp.transpose(pack[...])
    mass = own[48:56, :]
    volume = 1.0 / (1.0 + 0.125 * table[0:8, :])
    summed_mass = mass + 0.125 * table[8:16, :]
    rated = volume / mass
    for number, (ix, iy, iz) in enumerate(LEAVES):
        ratio[1 + ix, 1 + iy, 1 + iz] = rated[number : number + 1, :]
    exchange(ratio, devices, send_sems.at[1], recv_sems.at[1], EVERY)

    def finish_state(numbers):
        gather((2, 3), numbers)
        table[...] = jnp.transpose(pack[...])
        density = summed_mass / (volume + 0.125 * table[16:24, :])
        sticky = jnp.maximum(1.25 * table[24:32, :], 0.0)
        specific = (2.0 / 3.0) * own[56:64, :] / density
        for number in numbers:
            place = tuple(1 + i for i in LEAVES[number])
            for f, rows in enumerate((density, sticky, specific)):
                row = rows[number : number + 1, :]
                state[place + (slice(f, f + 1),)] = row
                own[8 * f + number : 8 * f + number + 1, :] = row
            state[place + (slice(3, 4),)] = jnp.zeros((1, 128), F32)

    second_pass([(0, INSIDE), (1, INSIDE)], fresh=True)
    await_leaves(40, ghost_ratio, recv_sems.at[1, 1])
    second_pass([(0, BESIDE), (1, BESIDE + BEYOND)])
    finish_state(upper)
    exchange(state, devices, send_sems.at[2], recv_sems.at[2], [i for i in EVERY if i < UPWARD])
    await_leaves(16, ghost_ratio, recv_sems.at[1, 0])
    second_pass([(0, BEYOND)])
    finish_state(lower)
    exchange(state, devices, send_sems.at[2], recv_sems.at[2], [i for i in EVERY if i >= UPWARD])

    turned = jnp.transpose(own[...])
    for f in range(3):
        for number in range(8):
            column = 8 * f + number
            far_columns[f, number] = jnp.broadcast_to(turned[:, column : column + 1], (128, 128))

    third_pass([(0, INSIDE), (1, INSIDE)], fresh=True)
    await_leaves(40, ghost_state, recv_sems.at[2, 1])
    third_pass([(0, BESIDE), (1, BESIDE + BEYOND)])
    gather(range(5), upper, fresh=True)
    await_leaves(16, ghost_state, recv_sems.at[2, 0])
    third_pass([(0, BEYOND)])
    gather(range(5), lower)
    table[...] = jnp.transpose(pack[...])

    for number, (ix, iy, iz) in enumerate(LEAVES):
        valid = own[64 + number : 65 + number, :] > 0.5
        total = table[number : number + 1, :]
        for d in range(3):
            row = 8 * (1 + d) + number
            spot = placed[1 + ix, 1 + iy, 1 + iz, d : d + 1, :]
            value = 1.25 * (spot * total - table[row : row + 1, :])
            accel_ref[ix, iy, d, iz : iz + 1, :] = jnp.where(valid, value, 0.0)
        rate_ref[ix, iy, iz : iz + 1, :] = jnp.where(
            valid, 1.25 * table[32 + number : 33 + number, :], 0.0
        )
    for phase, like in enumerate((ghost_base, ghost_ratio, ghost_state)):
        await_leaves(56, like, send_sems.at[phase])


def shards(offsets, velocity, mass, energy, partner_mask, counts):
    vmem = pl.BlockSpec(memory_space=pltpu.VMEM)
    smem = pl.BlockSpec(memory_space=pltpu.SMEM)
    offsets = jnp.transpose(offsets, (0, 1, 3, 2, 4))
    velocity = jnp.transpose(velocity, (0, 1, 3, 2, 4))
    acceleration, rate = pl.pallas_call(
        kernel,
        out_shape=(
            jax.ShapeDtypeStruct(offsets.shape, F32),
            jax.ShapeDtypeStruct(mass.shape, F32),
        ),
        in_specs=[vmem] * 4 + [smem] * 2,
        out_specs=(vmem, vmem),
        scratch_shapes=[
            pltpu.VMEM((4, 4, 4, 8, 128), F32),
            pltpu.VMEM((4, 4, 4, 8, 128), F32),
            pltpu.VMEM((4, 4, 4, 1, 128), F32),
            pltpu.VMEM((4, 4, 4, 4, 128), F32),
            pltpu.VMEM((128, 128), F32),
            pltpu.VMEM((8, 128, DEPTH), BF16),
            pltpu.VMEM((4, 4, 4, DEPTH, 256), BF16),
            pltpu.VMEM((3, 8, 128, 128), F32),
            pltpu.VMEM((5, 8, 128, 128), F32),
            pltpu.VMEM((8, 27, 128, 128), F32),
            pltpu.VMEM((8, 27, 128, 128), F32),
            pltpu.VMEM((8, 27, 128, 128), F32),
            pltpu.VMEM((128, 128), F32),
            pltpu.VMEM((128, 128), F32),
            pltpu.VMEM((56, 8, 128), F32),
            pltpu.VMEM((56, 1, 128), F32),
            pltpu.VMEM((56, 4, 128), F32),
            pltpu.SemaphoreType.DMA((3,)),
            pltpu.SemaphoreType.DMA((3, 2)),
        ],
        compiler_params=pltpu.CompilerParams(
            collective_id=0,
            has_side_effects=True,
            vmem_limit_bytes=60 * 1024 * 1024,
        ),
    )(offsets, velocity, mass, energy, partner_mask, counts)
    return jnp.transpose(acceleration, (0, 1, 3, 2, 4)), rate


def solution(mesh):
    placed = (
        P("gx", "gy", "gz", None, None),
        P("gx", "gy", "gz", None, None),
        P("gx", "gy", "gz", None),
        P("gx", "gy", "gz", None),
        P("gx", "gy", "gz", None),
        P("gx", "gy", "gz"),
    )
    return jax.shard_map(
        shards,
        mesh=mesh,
        in_specs=placed,
        out_specs=(P("gx", "gy", "gz", None, None), P("gx", "gy", "gz", None)),
        check_vma=False,
    )
```
